32 devices in a mesh: blk: 8 (over z, y), dir: 4 (over x, core).
Axes of the slice: x: 2, y: 2, z: 4, core: 2. Of those that a mesh axis runs over, the one named last changes fastest.
Arguments:
- spectrum: float32 [36, 36, 128, 128], P('dir', None, 'blk'), may hold values from 0 to 4.5, as said below
- group_speed: float32 [36, 128, 128], P(None, 'blk'), may hold values from 0.3 to 1
- ocean_current: float32 [2, 128, 128], P(None, 'blk'), may hold values from -0.5 to 0.5
- route_slot: int32 [128, 128], P('blk'), may hold values from -1 to 2047, as said below
- wind_vector: float32 [8, 2, 2048], P('blk'), may hold values from -4 to 4
- ice_cover: float32 [8, 2048], P('blk'), may hold values from 0 to 0.9
Outputs:
- spectrum_out: float32 [36, 36, 128, 128], P('dir', None, 'blk')
- ocean_forcing: float32 [4, 128, 128], P('dir', 'blk')
The draws below stay inside these ranges and needn't reach their ends.
Inputs may be any that keep to these rules, and one draw needn't show every extreme that they name: `route_slot`: on one geographic block the sea cells routed to one owner use slots 0 to their count - 1, at most 256 of them; some owner receives 256 cells from every block. Land cells hold -1. `spectrum`: positive everywhere.
All inputs are finite; a program needn't handle non-finite values.
Results may differ from the reference program's by a relative error of at most 0.00002.
Values sent between devices are 32-bit elements; how exact they have to be, the bound alone decides.
A program may use at most 64 MiB of HBM per device.

```python
import math
import jax
import jax.numpy as jnp
from jax import lax

DIRS = 36
FREQS = 36
GY = 128
CX = 16
BLOCKS = 8
NX = 128
CAP = 256
SLOTS = 2048


def draw_spectrum(key, part):
    cell_key, element_key = jax.random.split(jax.random.fold_in(key, 23))
    ramp = jnp.arange(DIRS, dtype=jnp.float32) / (DIRS - 1)
    cell_scale = jnp.exp(jax.random.uniform(cell_key, (NX, GY), jnp.float32, 0.0, math.log(10.0))) / 10.0
    element = jnp.exp(jax.random.uniform(element_key, (DIRS, FREQS, NX, GY), jnp.float32, math.log(0.1), 0.0))
    band = (1.0 + 2.0 * ramp)[:, None] * jnp.ones((FREQS,), jnp.float32)[None, :]
    return (band[:, :, None, None] * cell_scale[None, None] * element).astype(jnp.float32)


def draw_route_slot(key, part):
    target_key, block_keys = jax.random.split(jax.random.fold_in(key, 11))
    target = jax.random.randint(target_key, (), 0, BLOCKS)
    cell_count = CX * GY
    owners = jnp.arange(BLOCKS, dtype=jnp.int32)

    def one_block(block_index):
        block_key = jax.random.fold_in(block_keys, block_index)
        count_key, order_key = jax.random.split(block_key)
        counts = jax.random.randint(count_key, (BLOCKS,), 1, CAP + 1)
        counts = jnp.where(owners == target, CAP, counts).astype(jnp.int32)
        upper = jnp.cumsum(counts).astype(jnp.int32)
        lower = upper - counts
        ranks = jax.random.permutation(order_key, cell_count).astype(jnp.int32)
        owner = jnp.sum((ranks[:, None] >= upper[None, :]).astype(jnp.int32), axis=1)
        start = jnp.sum(jnp.where(owners[None, :] == owner[:, None], lower[None, :], 0), axis=1)
        routed = jnp.where(ranks < upper[BLOCKS - 1], owner * CAP + ranks - start, -1)
        return routed.reshape(CX, GY).astype(jnp.int32)
    return lax.map(one_block, owners).reshape(BLOCKS * CX, GY).astype(jnp.int32)


def shard_levels(key, shape, pieces, low, top_value):
    def one(dim, shards_of):
        steps = jax.random.uniform(jax.random.fold_in(jax.random.fold_in(key, 6), dim), (shards_of,), jnp.float32, low / len(pieces), top_value / len(pieces))
        return jnp.repeat(jnp.exp(steps), shape[dim] // shards_of).reshape((-1,) + (1,) * (len(shape) - dim - 1))

    factor_of = one(*pieces[0])
    for cut in pieces[1:]:
        factor_of = factor_of * one(*cut)
    return factor_of


def centred(stream_key, extent, spread, bound, pieces=(), kind=jnp.bfloat16):
    entries = jax.random.normal(stream_key, extent, jnp.float32) * spread
    if len(pieces) > 0:
        entries = shard_levels(stream_key, extent, pieces, -0.22, 0.18) * entries
    return jnp.clip(entries, min=-bound, max=bound).astype(kind)


def setup_inputs(seed: int = 0) -> dict:
    seeds = jax.random.split(jax.random.key(seed), 7)
    spectrum = draw_spectrum(jax.random.fold_in(seeds[6], 71), 0)
    group_speed = jnp.clip(0.3 + 0.7 * jax.random.uniform(seeds[1], (FREQS, NX, GY), jnp.float32) ** shard_levels(seeds[1], (FREQS, NX, GY), ((1, 8),), -0.2, 0.2), 0.3, 1.0)
    ocean_current = jnp.clip(jax.random.uniform(seeds[2], (2, GY, NX), jnp.float32, -0.5, 0.5) * shard_levels(seeds[2], (2, GY, NX), ((1, 8),), -0.4, 0.0), -0.5, 0.5)
    route_slot = draw_route_slot(jax.random.fold_in(seeds[6], 71), 0)
    wind_vector = centred(seeds[4], (BLOCKS, 2, SLOTS), 1.0, 4.0, ((0, 8),), jnp.float32)
    ice_cover = jnp.clip(0.9 * jax.random.uniform(seeds[5], (BLOCKS, SLOTS), jnp.float32) ** shard_levels(seeds[5], (BLOCKS, SLOTS), ((0, 8),), -0.2, 0.2), 0.0, 0.9)
    return {"spectrum": spectrum, "group_speed": group_speed, "ocean_current": ocean_current, "route_slot": route_slot, "wind_vector": wind_vector, "ice_cover": ice_cover}


COURANT = 0.15
WIND_GROWTH = 0.15
DAMP_RATE = 0.5
STEEP_COEF = 0.01
STRESS_SCALE = 1.0
STOKES_SCALE = 0.15
RATIO_STEP = 1.1


def flux_difference(energy, velocity, open_mask, along):
    count = energy.shape[along] - 1
    low_energy = lax.slice_in_dim(energy, 0, count, axis=along)
    high_energy = lax.slice_in_dim(energy, 1, count + 1, axis=along)
    face_speed = 0.5 * (lax.slice_in_dim(velocity, 0, count, axis=along) + lax.slice_in_dim(velocity, 1, count + 1, axis=along))
    face_open = lax.slice_in_dim(open_mask, 0, count, axis=along) * lax.slice_in_dim(open_mask, 1, count + 1, axis=along)
    flux = face_open * (jnp.maximum(face_speed, 0.0) * low_energy + jnp.minimum(face_speed, 0.0) * high_energy)
    return lax.slice_in_dim(flux, 1, count, axis=along) - lax.slice_in_dim(flux, 0, count - 1, axis=along)


def pad_edges(array, along):
    widths = [(0, 0)] * array.ndim
    widths[along] = (1, 1)
    return jnp.pad(array, widths)


def reference(spectrum, group_speed, ocean_current, route_slot, wind_vector, ice_cover):
    currents = jnp.transpose(ocean_current, (0, 2, 1))
    sea_mask = (route_slot >= 0).astype(jnp.float32)
    safe_slot = jnp.where(route_slot >= 0, route_slot, 0).astype(jnp.int32)
    owner = (safe_slot // CAP).astype(jnp.int32)
    column = ((jnp.arange(NX, dtype=jnp.int32) // CX)[:, None] * CAP + safe_slot % CAP).astype(jnp.int32)
    wind_cell = jnp.moveaxis(wind_vector[owner, :, column], -1, 0)
    ice_cell = ice_cover[owner, column]
    ratios = jnp.power(jnp.float32(RATIO_STEP), jnp.arange(FREQS, dtype=jnp.float32) - (FREQS - 1))
    ratio_square = ratios * ratios
    ratio_cube = ratio_square * ratios
    angles = 2.0 * jnp.pi * jnp.arange(DIRS, dtype=jnp.float32) / DIRS
    cosine_dir = jnp.cos(angles)
    sine_dir = jnp.sin(angles)

    def advect(inputs):
        energy, cosine, sine = inputs
        velocity_x = group_speed * cosine + currents[0]
        velocity_y = group_speed * sine + currents[1]
        mask_full = jnp.broadcast_to(sea_mask, energy.shape)
        div_x = flux_difference(pad_edges(energy, 1), pad_edges(velocity_x, 1), pad_edges(mask_full, 1), 1)
        div_y = flux_difference(pad_edges(energy, 2), pad_edges(velocity_y, 2), pad_edges(mask_full, 2), 2)
        return sea_mask * (energy - COURANT * (div_x + div_y))

    moved = lax.map(advect, (spectrum, cosine_dir, sine_dir))
    moment = jnp.sum(moved * ratio_square[None, :, None, None], axis=(0, 1))
    steepness = STEEP_COEF * moment
    damping = DAMP_RATE * steepness / (1.0 + steepness)

    def source(inputs):
        energy, cosine, sine = inputs
        wind_gain = WIND_GROWTH * (1.0 - ice_cell) * jnp.maximum(wind_cell[0] * cosine + wind_cell[1] * sine, 0.0)
        growth = ratios[:, None, None] * (wind_gain - damping)[None]
        updated = energy * (1.0 + growth)
        stress = jnp.sum(ratio_square[:, None, None] * wind_gain[None] * energy, axis=0)
        stokes = jnp.sum(ratio_cube[:, None, None] * updated, axis=0)
        return updated, stress, stokes

    updated, stress, stokes = lax.map(source, (moved, cosine_dir, sine_dir))
    cosine_full = cosine_dir[:, None, None]
    sine_full = sine_dir[:, None, None]
    forcing = jnp.stack([
        STRESS_SCALE * jnp.sum(cosine_full * stress, axis=0),
        STRESS_SCALE * jnp.sum(sine_full * stress, axis=0),
        STOKES_SCALE * jnp.sum(cosine_full * stokes, axis=0),
        STOKES_SCALE * jnp.sum(sine_full * stokes, axis=0)])
    return updated, jnp.transpose(forcing, (0, 2, 1))
```

```python
import functools
import math

import jax
import jax.numpy as jnp
import numpy as np
from jax import lax
from jax.experimental import pallas as pl
from jax.experimental.pallas import tpu as pltpu
from jax.sharding import PartitionSpec as P

COURANT = 0.15
WIND_GROWTH = 0.15
DAMP_RATE = 0.5
STEEP_COEF = 0.01
STRESS_SCALE = 1.0
STOKES_SCALE = 0.15
RATIO_STEP = 1.1
LANES = 128
MESH = pl.DeviceIdType.MESH


def moved_and_sums(
    shape,
    trig_ref, ratio_ref, spec_hbm, speed_ref, ocean_ref, route_ref, wind_ref, ice_ref,
    moved_hbm, gain_ref, damp_ref, force_ref,
    spec, moved, face_x, face_y, edge_out, edge_in, side_out, side_in,
    ocean_in, ocean_yx, ocean_xy, wind_in, ice_in, table, sums, part, part_in, stage, force_in,
    load_sem, store_sem, edge_send, edge_recv, side_send, side_recv,
    ocean_send, ocean_recv, wind_send, wind_recv, ice_send, ice_recv,
    part_send, part_recv, force_send, force_recv,
):
    blocks, bands, dirs, freqs, rows, yrows, chunk = shape
    width = rows * freqs
    b = lax.axis_index("blk")
    d = lax.axis_index("dir")
    capacity = rows * LANES // blocks
    wide = max(capacity, LANES)
    tiles = wide // LANES
    chunks = dirs // chunk

    def load(j):
        return pltpu.make_async_copy(spec_hbm.at[j], spec.at[j], load_sem.at[j])

    for j in range(dirs):
        load(j).start()

    barrier = pltpu.get_barrier_semaphore()

    def greet_blk(o, carry):
        pl.semaphore_signal(
            barrier, inc=1, device_id=(lax.rem(b + o, blocks), d), device_id_type=MESH
        )
        return carry

    lax.fori_loop(1, blocks, greet_blk, 0)
    for o in range(1, bands):
        pl.semaphore_signal(
            barrier, inc=1, device_id=(b, lax.rem(d + o, bands)), device_id_type=MESH
        )

    sea = jnp.where(route_ref[...] >= 0, 1.0, 0.0).astype(jnp.float32)
    for side, row in ((0, rows - 1), (1, 0)):
        side_out[side, :freqs, :] = speed_ref[pl.ds(row, freqs, stride=rows), :]
        side_out[side, freqs : freqs + 1, :] = sea[row : row + 1, :]

    @pl.when(b == 0)
    def _():
        side_in[0] = jnp.zeros_like(side_in[0])
        edge_in[0] = jnp.zeros_like(edge_in[0])

    @pl.when(b == blocks - 1)
    def _():
        side_in[1] = jnp.zeros_like(side_in[1])
        edge_in[1] = jnp.zeros_like(edge_in[1])

    pl.semaphore_wait(barrier, blocks - 1 + bands - 1)

    def ocean_copy(to, src, slot):
        return pltpu.make_async_remote_copy(
            src_ref=ocean_ref, dst_ref=ocean_in.at[src], send_sem=ocean_send.at[slot],
            recv_sem=ocean_recv.at[src], device_id=(to, d), device_id_type=MESH,
        )

    def wind_copy(to, src, slot):
        start = pl.multiple_of(((to * capacity) // LANES) * LANES, LANES)
        return pltpu.make_async_remote_copy(
            src_ref=wind_ref.at[0, :, pl.ds(start, wide)], dst_ref=wind_in.at[src],
            send_sem=wind_send.at[slot], recv_sem=wind_recv.at[src],
            device_id=(to, d), device_id_type=MESH,
        )

    def ice_copy(to, src, slot):
        start = pl.multiple_of(((to * capacity) // LANES) * LANES, LANES)
        return pltpu.make_async_remote_copy(
            src_ref=ice_ref.at[:, pl.ds(start, wide)], dst_ref=ice_in.at[src],
            send_sem=ice_send.at[slot], recv_sem=ice_recv.at[src],
            device_id=(to, d), device_id_type=MESH,
        )

    def send_ocean(o, carry):
        ocean_copy(lax.rem(b + o, blocks), b, o).start()
        return carry

    def send_winds(o, carry):
        to = lax.rem(b + o, blocks)
        wind_copy(to, b, o).start()
        ice_copy(to, b, o).start()
        return carry

    lax.fori_loop(1, blocks, send_ocean, 0)

    def side_copy(side):
        return pltpu.make_async_remote_copy(
            src_ref=side_out.at[side], dst_ref=side_in.at[side], send_sem=side_send.at[side],
            recv_sem=side_recv.at[side], device_id=(b + 1 - 2 * side, d), device_id_type=MESH,
        )

    def edge_copy(side, c):
        part_of = pl.ds(c * chunk, chunk)
        return pltpu.make_async_remote_copy(
            src_ref=edge_out.at[side, part_of], dst_ref=edge_in.at[side, part_of],
            send_sem=edge_send.at[side, c], recv_sem=edge_recv.at[side, c],
            device_id=(b + 1 - 2 * side, d), device_id_type=MESH,
        )

    sends = ((0, b < blocks - 1), (1, b > 0))
    receives = ((0, b > 0), (1, b < blocks - 1))
    for side, has in sends:
        @pl.when(has)
        def _(side=side):
            side_copy(side).start()

    for c in range(chunks):
        for j in range(c * chunk, (c + 1) * chunk):
            load(j).wait()
            for side, row in ((0, rows - 1), (1, 0)):
                edge_out[side, j] = spec[j, pl.ds(row, freqs, stride=rows), :]
        for side, has in sends:
            @pl.when(has)
            def _(side=side, c=c):
                edge_copy(side, c).start()

    lax.fori_loop(1, blocks, send_winds, 0)

    row_id = lax.broadcasted_iota(jnp.int32, (rows, LANES), 0)
    lane_id = lax.broadcasted_iota(jnp.int32, (rows, LANES), 1)

    def next_row(value):
        return pltpu.roll(value, rows - 1, 0)

    def next_lane(value):
        return pltpu.roll(value, LANES - 1, 1)

    half = 0.5 * COURANT
    open_x = jnp.where(row_id < rows - 1, half * sea * next_row(sea), 0.0)
    open_y = jnp.where(lane_id < LANES - 1, half * sea * next_lane(sea), 0.0)

    def faces(k, carry):
        at = pl.ds(pl.multiple_of(k * rows, rows), rows)
        speed = speed_ref[at, :]
        face_x[at, :] = open_x * (speed + next_row(speed))
        face_y[at, :] = open_y * (speed + next_lane(speed))
        return carry

    lax.fori_loop(0, freqs, faces, 0, unroll=4)

    ocean_in[b] = ocean_ref[...]

    def wait_ocean(o, carry):
        ocean_copy(lax.rem(b + o, blocks), lax.rem(b + o, blocks), o).wait_recv()
        return carry

    lax.fori_loop(1, blocks, wait_ocean, 0)

    def lay_ocean(i, carry):
        at = i * yrows
        if yrows % 8 == 0:
            at = pl.multiple_of(at, 8)
        for comp in range(2):
            ocean_yx[comp, pl.ds(at, yrows), :] = ocean_in[i, comp]
        return carry

    lax.fori_loop(0, blocks, lay_ocean, 0)
    ocean_xy[:, 0:8, :] = jnp.zeros((2, 8, LANES), jnp.float32)
    total = blocks * rows
    ocean_xy[:, total + 8 : total + 16, :] = jnp.zeros((2, 8, LANES), jnp.float32)
    for comp in range(2):
        for t in range(total // LANES):
            ocean_xy[comp, 8 + t * LANES : 8 + (t + 1) * LANES, :] = jnp.transpose(
                ocean_yx[comp, :, t * LANES : (t + 1) * LANES]
            )
    own = pl.ds(pl.multiple_of(b * rows + 8, 8), rows)
    flow_x = ocean_xy[0, own, :]
    flow_y = ocean_xy[1, own, :]
    flow_low = ocean_xy[0, pl.ds(b * rows + 7, 1), :]
    flow_high = ocean_xy[0, pl.ds(b * rows + 8 + rows, 1), :]
    cur_x = open_x * (flow_x + next_row(flow_x))
    cur_y = open_y * (flow_y + next_lane(flow_y))

    group = 1
    for size in (6, 5, 4, 3, 2):
        if freqs % size == 0:
            group = size
            break

    def one_dir(j, carry):
        cosine = trig_ref[0, d * dirs + j]
        sine = trig_ref[1, d * dirs + j]

        def some_freqs(g, acc):
            two, three, four = acc
            for i in range(group):
                k = g * group + i
                at = pl.ds(pl.multiple_of(k * rows, rows), rows)
                energy = spec[j, at, :]
                speed_x = face_x[at, :] * cosine + cur_x
                flux_x = speed_x * jnp.where(speed_x > 0.0, energy, next_row(energy))
                speed_y = face_y[at, :] * sine + cur_y
                flux_y = speed_y * jnp.where(speed_y > 0.0, energy, next_lane(energy))
                value = (
                    sea * energy - (flux_x - pltpu.roll(flux_x, 1, 0))
                ) - (flux_y - pltpu.roll(flux_y, 1, 1))
                moved[j, at, :] = value
                two = two + ratio_ref[0, k] * value
                three = three + ratio_ref[1, k] * value
                four = four + ratio_ref[2, k] * value
            return two, three, four

        zero = jnp.zeros((rows, LANES), jnp.float32)
        acc = lax.fori_loop(0, freqs // group, some_freqs, (zero, zero, zero))
        for i in range(3):
            sums[j, i] = acc[i]
        return carry

    lax.fori_loop(0, dirs, one_dir, 0)

    high = blocks * tiles
    own_lane = pl.multiple_of(((b * capacity) // LANES) * LANES, LANES)
    wind_in[b] = wind_ref[0, :, pl.ds(own_lane, wide)]
    ice_in[b] = ice_ref[:, pl.ds(own_lane, wide)]

    def wait_winds(o, carry):
        src = lax.rem(b + o, blocks)
        wind_copy(src, src, o).wait_recv()
        ice_copy(src, src, o).wait_recv()
        return carry

    lax.fori_loop(1, blocks, wait_winds, 0)

    def lay_table(i, carry):
        for t in range(tiles):
            lanes = slice(t * LANES, (t + 1) * LANES)
            for comp in range(2):
                table[pl.ds(comp * high + i * tiles + t, 1), :] = wind_in[i, comp : comp + 1, lanes]
            table[pl.ds(2 * high + i * tiles + t, 1), :] = ice_in[i, :, lanes]
        return carry

    lax.fori_loop(0, blocks, lay_table, 0)
    whole = table[...]
    first = whole.astype(jnp.bfloat16)
    rest = whole - first.astype(jnp.float32)
    second = rest.astype(jnp.bfloat16)
    third = (rest - second.astype(jnp.float32)).astype(jnp.bfloat16)
    entry_id = lax.broadcasted_iota(jnp.int32, (LANES, LANES), 0)
    high_id = lax.broadcasted_iota(jnp.int32, (high, LANES), 0)
    per_row = int(math.log2(min(capacity, LANES)))
    offset = lax.rem(b * capacity, LANES) if capacity < LANES else 0
    found = [[], [], []]
    for row in range(rows):
        slot = route_ref[row : row + 1, :]
        upper = lax.shift_right_arithmetic(slot, per_row)
        lower = jnp.bitwise_and(slot, (1 << per_row) - 1) + offset
        hot = jnp.where(entry_id == lower, 1.0, 0.0).astype(jnp.bfloat16)
        values = sum(
            jnp.dot(piece, hot, preferred_element_type=jnp.float32)
            for piece in (third, second, first)
        )
        here = high_id == upper
        for i in range(3):
            found[i].append(
                jnp.sum(
                    jnp.where(here, values[i * high : (i + 1) * high], 0.0), axis=0, keepdims=True
                )
            )
    wind_x, wind_y, ice = (jnp.concatenate(value, axis=0) for value in found)
    growth = WIND_GROWTH * (1.0 - ice)

    for side, has in receives:
        @pl.when(has)
        def _(side=side):
            side_copy(side).wait_recv()
    low_open = half * side_in[0, freqs : freqs + 1, :] * sea[0:1]
    high_open = half * side_in[1, freqs : freqs + 1, :] * sea[rows - 1 : rows]
    low_face = low_open * (side_in[0, :freqs, :] + side_out[1, :freqs, :])
    high_face = high_open * (side_in[1, :freqs, :] + side_out[0, :freqs, :])
    low_cur = low_open * (flow_low + flow_x[0:1])
    high_cur = high_open * (flow_high + flow_x[rows - 1 : rows])
    power = lax.broadcasted_iota(jnp.int32, (freqs, LANES), 0).astype(jnp.float32) - (freqs - 1)
    ratio = jnp.exp(power * math.log(RATIO_STEP))
    square = ratio * ratio
    weights = (square, square * ratio, square * square)

    zero = jnp.zeros((rows, LANES), jnp.float32)
    moment, stress_x, stress_y, base_x, base_y, damp_x, damp_y = [zero] * 7
    for c in range(chunks):
        for side, has in receives:
            @pl.when(has)
            def _(side=side, c=c):
                edge_copy(side, c).wait_recv()
        for j in range(c * chunk, (c + 1) * chunk):
            cosine = trig_ref[0, d * dirs + j]
            sine = trig_ref[1, d * dirs + j]
            low_speed = low_face * cosine + low_cur
            high_speed = high_face * cosine + high_cur
            low_flux = low_speed * jnp.where(low_speed > 0.0, edge_in[0, j], edge_out[1, j])
            high_flux = high_speed * jnp.where(high_speed > 0.0, edge_out[0, j], edge_in[1, j])
            low_at = pl.ds(0, freqs, stride=rows)
            high_at = pl.ds(rows - 1, freqs, stride=rows)
            moved[j, low_at, :] = moved[j, low_at, :] + low_flux
            moved[j, high_at, :] = moved[j, high_at, :] - high_flux
            pltpu.make_async_copy(moved.at[j], moved_hbm.at[j], store_sem.at[j]).start()
            fixed = []
            for i in range(3):
                low_sum = jnp.sum(weights[i] * low_flux, axis=0, keepdims=True)
                high_sum = jnp.sum(weights[i] * high_flux, axis=0, keepdims=True)
                fixed.append(
                    sums[j, i]
                    + jnp.where(row_id == 0, low_sum, 0.0)
                    - jnp.where(row_id == rows - 1, high_sum, 0.0)
                )
            two, three, four = fixed
            gain = growth * jnp.maximum(wind_x * cosine + wind_y * sine, 0.0)
            gain_ref[j] = gain
            moment = moment + two
            stress = gain * two
            stress_x = stress_x + cosine * stress
            stress_y = stress_y + sine * stress
            base = three + gain * four
            base_x = base_x + cosine * base
            base_y = base_y + sine * base
            damp_x = damp_x + cosine * four
            damp_y = damp_y + sine * four

    pairs = (
        (STRESS_SCALE * stress_x, zero),
        (STRESS_SCALE * stress_y, zero),
        (STOKES_SCALE * base_x, STOKES_SCALE * damp_x),
        (STOKES_SCALE * base_y, STOKES_SCALE * damp_y),
    )
    for comp in range(4):
        part[comp, 0] = moment
        part[comp, 1] = pairs[comp][0]
        part[comp, 2] = pairs[comp][1]

    def part_copy(to, src, slot):
        return pltpu.make_async_remote_copy(
            src_ref=part.at[to], dst_ref=part_in.at[src], send_sem=part_send.at[slot],
            recv_sem=part_recv.at[src], device_id=(b, to), device_id_type=MESH,
        )

    for o in range(1, bands):
        part_copy(lax.rem(d + o, bands), d, o).start()
    part_in[d] = part[d]
    for o in range(1, bands):
        src = lax.rem(d + o, bands)
        part_copy(src, src, o).wait_recv()
    summed = part_in[0]
    for i in range(1, bands):
        summed = summed + part_in[i]
    steepness = STEEP_COEF * summed[0]
    damping = DAMP_RATE * steepness / (1.0 + steepness)
    damp_ref[...] = damping
    force = summed[1] - damping * summed[2]

    square_tile = jnp.concatenate([force, jnp.zeros((LANES - rows, LANES), jnp.float32)], axis=0)
    per_tile = LANES // rows
    stage[...] = jnp.transpose(
        pltpu.roll(square_tile, lax.rem(b, per_tile) * rows, 0)
    )
    if yrows % 8 == 0:
        def force_src(i):
            return stage.at[pl.ds(pl.multiple_of(i * yrows, 8), yrows)]
    else:
        def force_src(i):
            return force_in.at[blocks + i]

        def lay_force(i, carry):
            force_in[blocks + i] = stage[pl.ds(i * yrows, yrows), :]
            return carry

        lax.fori_loop(0, blocks, lay_force, 0)

    def force_copy(to, src, slot):
        return pltpu.make_async_remote_copy(
            src_ref=force_src(to), dst_ref=force_in.at[src], send_sem=force_send.at[slot],
            recv_sem=force_recv.at[src], device_id=(to, d), device_id_type=MESH,
        )

    def send_force(o, carry):
        force_copy(lax.rem(b + o, blocks), b, o).start()
        return carry

    def wait_force(o, carry):
        src = lax.rem(b + o, blocks)
        force_copy(src, src, o).wait_recv()
        return carry

    lax.fori_loop(1, blocks, send_force, 0)
    force_in[b] = stage[pl.ds(b * yrows if yrows % 8 else pl.multiple_of(b * yrows, 8), yrows), :]

    def drain(o, carry):
        to = lax.rem(b + o, blocks)
        ocean_copy(to, b, o).wait_send()
        wind_copy(to, b, o).wait_send()
        ice_copy(to, b, o).wait_send()
        return carry

    lax.fori_loop(1, blocks, drain, 0)
    for side, has in sends:
        @pl.when(has)
        def _(side=side):
            side_copy(side).wait_send()
            for c in range(chunks):
                edge_copy(side, c).wait_send()
    for o in range(1, bands):
        part_copy(lax.rem(d + o, bands), d, o).wait_send()
    for j in range(dirs):
        pltpu.make_async_copy(moved.at[j], moved_hbm.at[j], store_sem.at[j]).wait()

    lax.fori_loop(1, blocks, wait_force, 0)
    for t in range(blocks // per_tile):
        tile = force_in[t * per_tile]
        for i in range(1, per_tile):
            tile = tile + force_in[t * per_tile + i]
        force_ref[0, :, t * LANES : (t + 1) * LANES] = tile

    def drain_force(o, carry):
        force_copy(lax.rem(b + o, blocks), b, o).wait_send()
        return carry

    lax.fori_loop(1, blocks, drain_force, 0)


def on_device(spectrum, group_speed, ocean_current, route_slot, wind_vector, ice_cover):
    blocks = lax.axis_size("blk")
    bands = lax.axis_size("dir")
    dirs, freqs, rows, width = spectrum.shape
    yrows = ocean_current.shape[1]
    capacity = rows * width // blocks
    wide = max(capacity, LANES)
    chunk = 3 if dirs % 3 == 0 else 1
    chunks = dirs // chunk
    high = blocks * (wide // LANES)
    total = blocks * rows
    padded = (freqs // 8 + 1) * 8
    f32 = jnp.float32
    count = dirs * bands
    angles = 2.0 * np.pi * np.arange(count) / count
    trig = jnp.asarray(np.stack([np.cos(angles), np.sin(angles)]), f32)
    ratios = RATIO_STEP ** (np.arange(freqs) - (freqs - 1.0))
    ratio_table = jnp.asarray(np.stack([ratios**2, ratios**3, ratios**4]), f32)
    shape = (blocks, bands, dirs, freqs, rows, yrows, chunk)
    vmem = pl.BlockSpec(memory_space=pltpu.VMEM)
    smem = pl.BlockSpec(memory_space=pltpu.SMEM)
    anywhere = pl.BlockSpec(memory_space=pl.ANY)
    dma = pltpu.SemaphoreType.DMA
    force_slots = blocks if yrows % 8 == 0 else 2 * blocks
    moved, gain, damping, forcing = pl.pallas_call(
        functools.partial(moved_and_sums, shape),
        out_shape=(
            jax.ShapeDtypeStruct((dirs, freqs * rows, width), f32),
            jax.ShapeDtypeStruct((dirs, rows, width), f32),
            jax.ShapeDtypeStruct((rows, width), f32),
            jax.ShapeDtypeStruct((1, yrows, total), f32),
        ),
        in_specs=[smem, smem, anywhere, vmem, vmem, vmem, vmem, vmem],
        out_specs=(anywhere, vmem, vmem, vmem),
        scratch_shapes=[
            pltpu.VMEM((dirs, freqs * rows, width), f32),
            pltpu.VMEM((dirs, freqs * rows, width), f32),
            pltpu.VMEM((freqs * rows, width), f32),
            pltpu.VMEM((freqs * rows, width), f32),
            pltpu.VMEM((2, dirs, freqs, width), f32),
            pltpu.VMEM((2, dirs, freqs, width), f32),
            pltpu.VMEM((2, padded, width), f32),
            pltpu.VMEM((2, padded, width), f32),
            pltpu.VMEM((blocks, 2, yrows, total), f32),
            pltpu.VMEM((2, blocks * yrows, total), f32),
            pltpu.VMEM((2, total + 16, width), f32),
            pltpu.VMEM((blocks, 2, wide), f32),
            pltpu.VMEM((blocks, 1, wide), f32),
            pltpu.VMEM((3 * high, LANES), f32),
            pltpu.VMEM((dirs, 3, rows, width), f32),
            pltpu.VMEM((4, 3, rows, width), f32),
            pltpu.VMEM((bands, 3, rows, width), f32),
            pltpu.VMEM((width, LANES), f32),
            pltpu.VMEM((force_slots, yrows, LANES), f32),
            dma((dirs,)), dma((dirs,)),
            dma((2, chunks)), dma((2, chunks)), dma((2,)), dma((2,)),
            dma((blocks,)), dma((blocks,)), dma((blocks,)), dma((blocks,)),
            dma((blocks,)), dma((blocks,)),
            dma((bands,)), dma((bands,)), dma((blocks,)), dma((blocks,)),
        ],
        compiler_params=pltpu.CompilerParams(
            collective_id=0, has_side_effects=True, vmem_limit_bytes=48 * 1024 * 1024
        ),
        cost_estimate=pl.CostEstimate(
            flops=30 * spectrum.size, bytes_accessed=8 * spectrum.size, transcendentals=0
        ),
    )(
        trig, ratio_table, spectrum.reshape(dirs, freqs * rows, width),
        group_speed.reshape(freqs * rows, width), ocean_current, route_slot, wind_vector, ice_cover,
    )
    growth = jnp.asarray(ratios, f32)[None, :, None, None] * (gain - damping)[:, None]
    result = moved.reshape(dirs, freqs, rows, width) * (1.0 + growth)
    return result, forcing


def solution(mesh):
    return jax.shard_map(
        on_device,
        mesh=mesh,
        in_specs=(
            P("dir", None, "blk", None),
            P(None, "blk", None),
            P(None, "blk", None),
            P("blk", None),
            P("blk", None, None),
            P("blk", None),
        ),
        out_specs=(P("dir", None, "blk", None), P("dir", "blk", None)),
        check_vma=False,
    )
```

```python
import functools
import math

import jax
import jax.numpy as jnp
import numpy as np
from jax import lax
from jax.experimental import pallas as pl
from jax.experimental.pallas import tpu as pltpu
from jax.sharding import PartitionSpec as P

COURANT = 0.15
WIND_GROWTH = 0.15
DAMP_RATE = 0.5
STEEP_COEF = 0.01
STRESS_SCALE = 1.0
STOKES_SCALE = 0.15
RATIO_STEP = 1.1
LANES = 128
MESH = pl.DeviceIdType.MESH


def moved_and_sums(
    shape,
    spec_hbm, speed_hbm, ocean_hbm, route_hbm, wind_ref, ice_ref,
    moved, gain_ref, force_ref,
    trig_ref, ratio_ref, speed_ref, ocean_ref, route_ref,
    spec, face_x, face_y, edge_out, edge_in, side_out, side_in,
    ocean_in, ocean_yx, ocean_xy, wind_in, ice_in, table, sums, part, part_in, stage, force_in,
    load_sem, small_sem, edge_send, edge_recv, side_send, side_recv,
    ocean_send, ocean_recv, wind_send, wind_recv, ice_send, ice_recv,
    part_send, part_recv, force_send, force_recv,
):
    blocks, bands, dirs, freqs, rows, yrows, chunk = shape
    width = rows * freqs
    b = lax.axis_index("blk")
    d = lax.axis_index("dir")
    capacity = rows * LANES // blocks
    wide = max(capacity, LANES)
    tiles = wide // LANES
    chunks = dirs // chunk

    def load(j):
        return pltpu.make_async_copy(spec_hbm.at[j], spec.at[j], load_sem.at[j])

    small = [
        pltpu.make_async_copy(speed_hbm, speed_ref, small_sem.at[0]),
        pltpu.make_async_copy(route_hbm, route_ref, small_sem.at[1]),
        pltpu.make_async_copy(ocean_hbm, ocean_ref, small_sem.at[2]),
    ]
    for copy in small:
        copy.start()
    for j in range(dirs):
        load(j).start()
    own_lane = pl.multiple_of(((b * capacity) // LANES) * LANES, LANES)
    own_wind = pltpu.make_async_copy(
        wind_ref.at[0, :, pl.ds(own_lane, wide)], wind_in.at[b], small_sem.at[3]
    )
    own_ice = pltpu.make_async_copy(
        ice_ref.at[:, pl.ds(own_lane, wide)], ice_in.at[b], small_sem.at[4]
    )
    own_wind.start()
    own_ice.start()

    barrier = pltpu.get_barrier_semaphore()

    def greet_blk(o, carry):
        pl.semaphore_signal(
            barrier, inc=1, device_id=(lax.rem(b + o, blocks), d), device_id_type=MESH
        )
        return carry

    lax.fori_loop(1, blocks, greet_blk, 0)
    for o in range(1, bands):
        pl.semaphore_signal(
            barrier, inc=1, device_id=(b, lax.rem(d + o, bands)), device_id_type=MESH
        )

    count = dirs * bands
    for j in range(dirs):
        for i, wave in enumerate((math.cos, math.sin)):
            value = jnp.float32(wave(2.0 * math.pi * j / count))
            for band in range(1, bands):
                angle = 2.0 * math.pi * (band * dirs + j) / count
                value = jnp.where(d == band, jnp.float32(wave(angle)), value)
            trig_ref[i, j] = value
    for k in range(freqs):
        for i in range(3):
            ratio_ref[i, k] = jnp.float32(RATIO_STEP ** ((k - freqs + 1.0) * (i + 2)))

    for copy in small:
        copy.wait()
    sea = jnp.where(route_ref[...] >= 0, 1.0, 0.0).astype(jnp.float32)
    for side, row in ((0, rows - 1), (1, 0)):
        side_out[side, :freqs, :] = speed_ref[pl.ds(row, freqs, stride=rows), :]
        side_out[side, freqs : freqs + 1, :] = sea[row : row + 1, :]

    @pl.when(b == 0)
    def _():
        side_in[0] = jnp.zeros_like(side_in[0])
        edge_in[0] = jnp.zeros_like(edge_in[0])

    @pl.when(b == blocks - 1)
    def _():
        side_in[1] = jnp.zeros_like(side_in[1])
        edge_in[1] = jnp.zeros_like(edge_in[1])

    pl.semaphore_wait(barrier, blocks - 1 + bands - 1)

    def ocean_copy(to, src, slot):
        return pltpu.make_async_remote_copy(
            src_ref=ocean_hbm, dst_ref=ocean_in.at[src], send_sem=ocean_send.at[slot],
            recv_sem=ocean_recv.at[src], device_id=(to, d), device_id_type=MESH,
        )

    def wind_copy(to, src, slot):
        start = pl.multiple_of(((to * capacity) // LANES) * LANES, LANES)
        return pltpu.make_async_remote_copy(
            src_ref=wind_ref.at[0, :, pl.ds(start, wide)], dst_ref=wind_in.at[src],
            send_sem=wind_send.at[slot], recv_sem=wind_recv.at[src],
            device_id=(to, d), device_id_type=MESH,
        )

    def ice_copy(to, src, slot):
        start = pl.multiple_of(((to * capacity) // LANES) * LANES, LANES)
        return pltpu.make_async_remote_copy(
            src_ref=ice_ref.at[:, pl.ds(start, wide)], dst_ref=ice_in.at[src],
            send_sem=ice_send.at[slot], recv_sem=ice_recv.at[src],
            device_id=(to, d), device_id_type=MESH,
        )

    def send_ocean(o, carry):
        ocean_copy(lax.rem(b + o, blocks), b, o).start()
        return carry

    def send_winds(o, carry):
        to = lax.rem(b + o, blocks)
        wind_copy(to, b, o).start()
        ice_copy(to, b, o).start()
        return carry

    lax.fori_loop(1, blocks, send_ocean, 0)

    def side_copy(side):
        return pltpu.make_async_remote_copy(
            src_ref=side_out.at[side], dst_ref=side_in.at[side], send_sem=side_send.at[side],
            recv_sem=side_recv.at[side], device_id=(b + 1 - 2 * side, d), device_id_type=MESH,
        )

    def edge_copy(side, c):
        part_of = pl.ds(c * chunk, chunk)
        return pltpu.make_async_remote_copy(
            src_ref=edge_out.at[side, part_of], dst_ref=edge_in.at[side, part_of],
            send_sem=edge_send.at[side, c], recv_sem=edge_recv.at[side, c],
            device_id=(b + 1 - 2 * side, d), device_id_type=MESH,
        )

    sends = ((0, b < blocks - 1), (1, b > 0))
    receives = ((0, b > 0), (1, b < blocks - 1))
    for side, has in sends:
        @pl.when(has)
        def _(side=side):
            side_copy(side).start()

    for c in range(chunks):
        for j in range(c * chunk, (c + 1) * chunk):
            load(j).wait()
            for side, row in ((0, rows - 1), (1, 0)):
                edge_out[side, j] = spec[j, pl.ds(row, freqs, stride=rows), :]
        for side, has in sends:
            @pl.when(has)
            def _(side=side, c=c):
                edge_copy(side, c).start()

    lax.fori_loop(1, blocks, send_winds, 0)

    row_id = lax.broadcasted_iota(jnp.int32, (rows, LANES), 0)
    lane_id = lax.broadcasted_iota(jnp.int32, (rows, LANES), 1)

    def next_row(value):
        return pltpu.roll(value, rows - 1, 0)

    def next_lane(value):
        return pltpu.roll(value, LANES - 1, 1)

    half = 0.5 * COURANT
    open_x = jnp.where(row_id < rows - 1, half * sea * next_row(sea), 0.0)
    open_y = jnp.where(lane_id < LANES - 1, half * sea * next_lane(sea), 0.0)

    def faces(k, carry):
        at = pl.ds(pl.multiple_of(k * rows, rows), rows)
        speed = speed_ref[at, :]
        face_x[at, :] = open_x * (speed + next_row(speed))
        face_y[at, :] = open_y * (speed + next_lane(speed))
        return carry

    lax.fori_loop(0, freqs, faces, 0, unroll=4)

    ocean_in[b] = ocean_ref[...]

    def wait_ocean(o, carry):
        ocean_copy(lax.rem(b + o, blocks), lax.rem(b + o, blocks), o).wait_recv()
        return carry

    lax.fori_loop(1, blocks, wait_ocean, 0)

    def lay_ocean(i, carry):
        at = i * yrows
        if yrows % 8 == 0:
            at = pl.multiple_of(at, 8)
        for comp in range(2):
            ocean_yx[comp, pl.ds(at, yrows), :] = ocean_in[i, comp]
        return carry

    lax.fori_loop(0, blocks, lay_ocean, 0)
    ocean_xy[:, 0:8, :] = jnp.zeros((2, 8, LANES), jnp.float32)
    total = blocks * rows
    ocean_xy[:, total + 8 : total + 16, :] = jnp.zeros((2, 8, LANES), jnp.float32)
    for comp in range(2):
        for t in range(total // LANES):
            ocean_xy[comp, 8 + t * LANES : 8 + (t + 1) * LANES, :] = jnp.transpose(
                ocean_yx[comp, :, t * LANES : (t + 1) * LANES]
            )
    own = pl.ds(pl.multiple_of(b * rows + 8, 8), rows)
    flow_x = ocean_xy[0, own, :]
    flow_y = ocean_xy[1, own, :]
    flow_low = ocean_xy[0, pl.ds(b * rows + 7, 1), :]
    flow_high = ocean_xy[0, pl.ds(b * rows + 8 + rows, 1), :]
    cur_x = open_x * (flow_x + next_row(flow_x))
    cur_y = open_y * (flow_y + next_lane(flow_y))

    group = 1
    for size in (12, 9, 6, 4, 3, 2):
        if freqs % size == 0:
            group = size
            break

    def one_dir(j, carry):
        cosine = trig_ref[0, j]
        sine = trig_ref[1, j]

        def some_freqs(g, acc):
            two, three, four = acc
            for i in range(group):
                k = g * group + i
                at = pl.ds(pl.multiple_of(k * rows, rows), rows)
                energy = spec[j, at, :]
                speed_x = face_x[at, :] * cosine + cur_x
                flux_x = speed_x * jnp.where(speed_x > 0.0, energy, next_row(energy))
                speed_y = face_y[at, :] * sine + cur_y
                flux_y = speed_y * jnp.where(speed_y > 0.0, energy, next_lane(energy))
                value = (
                    sea * energy - (flux_x - pltpu.roll(flux_x, 1, 0))
                ) - (flux_y - pltpu.roll(flux_y, 1, 1))
                moved[j, at, :] = value
                two = two + ratio_ref[0, k] * value
                three = three + ratio_ref[1, k] * value
                four = four + ratio_ref[2, k] * value
            return two, three, four

        zero = jnp.zeros((rows, LANES), jnp.float32)
        acc = lax.fori_loop(0, freqs // group, some_freqs, (zero, zero, zero))
        for i in range(3):
            sums[j, i] = acc[i]
        return carry

    lax.fori_loop(0, dirs, one_dir, 0)

    high = blocks * tiles
    own_wind.wait()
    own_ice.wait()

    def wait_winds(o, carry):
        src = lax.rem(b + o, blocks)
        wind_copy(src, src, o).wait_recv()
        ice_copy(src, src, o).wait_recv()
        return carry

    lax.fori_loop(1, blocks, wait_winds, 0)

    def lay_table(i, carry):
        for t in range(tiles):
            lanes = slice(t * LANES, (t + 1) * LANES)
            for comp in range(2):
                table[pl.ds(comp * high + i * tiles + t, 1), :] = wind_in[i, comp : comp + 1, lanes]
            table[pl.ds(2 * high + i * tiles + t, 1), :] = ice_in[i, :, lanes]
        return carry

    lax.fori_loop(0, blocks, lay_table, 0)
    whole = table[...]
    first = whole.astype(jnp.bfloat16)
    rest = whole - first.astype(jnp.float32)
    second = rest.astype(jnp.bfloat16)
    third = (rest - second.astype(jnp.float32)).astype(jnp.bfloat16)
    entry_id = lax.broadcasted_iota(jnp.int32, (LANES, LANES), 0)
    high_id = lax.broadcasted_iota(jnp.int32, (high, LANES), 0)
    per_row = int(math.log2(min(capacity, LANES)))
    offset = lax.rem(b * capacity, LANES) if capacity < LANES else 0
    found = [[], [], []]
    for row in range(rows):
        slot = route_ref[row : row + 1, :]
        upper = lax.shift_right_arithmetic(slot, per_row)
        lower = jnp.bitwise_and(slot, (1 << per_row) - 1) + offset
        hot = jnp.where(entry_id == lower, 1.0, 0.0).astype(jnp.bfloat16)
        values = sum(
            jnp.dot(piece, hot, preferred_element_type=jnp.float32)
            for piece in (third, second, first)
        )
        here = high_id == upper
        for i in range(3):
            found[i].append(
                jnp.sum(
                    jnp.where(here, values[i * high : (i + 1) * high], 0.0), axis=0, keepdims=True
                )
            )
    wind_x, wind_y, ice = (jnp.concatenate(value, axis=0) for value in found)
    growth = WIND_GROWTH * (1.0 - ice)

    for side, has in receives:
        @pl.when(has)
        def _(side=side):
            side_copy(side).wait_recv()
    low_open = half * side_in[0, freqs : freqs + 1, :] * sea[0:1]
    high_open = half * side_in[1, freqs : freqs + 1, :] * sea[rows - 1 : rows]
    low_face = low_open * (side_in[0, :freqs, :] + side_out[1, :freqs, :])
    high_face = high_open * (side_in[1, :freqs, :] + side_out[0, :freqs, :])
    low_cur = low_open * (flow_low + flow_x[0:1])
    high_cur = high_open * (flow_high + flow_x[rows - 1 : rows])
    power = lax.broadcasted_iota(jnp.int32, (freqs, LANES), 0).astype(jnp.float32) - (freqs - 1)
    ratio = jnp.exp(power * math.log(RATIO_STEP))
    square = ratio * ratio
    weights = (square, square * ratio, square * square)

    zero = jnp.zeros((rows, LANES), jnp.float32)
    moment, stress_x, stress_y, base_x, base_y, damp_x, damp_y = [zero] * 7
    for c in range(chunks):
        for side, has in receives:
            @pl.when(has)
            def _(side=side, c=c):
                edge_copy(side, c).wait_recv()
        for j in range(c * chunk, (c + 1) * chunk):
            cosine = trig_ref[0, j]
            sine = trig_ref[1, j]
            low_speed = low_face * cosine + low_cur
            high_speed = high_face * cosine + high_cur
            low_flux = low_speed * jnp.where(low_speed > 0.0, edge_in[0, j], edge_out[1, j])
            high_flux = high_speed * jnp.where(high_speed > 0.0, edge_out[0, j], edge_in[1, j])
            low_at = pl.ds(0, freqs, stride=rows)
            high_at = pl.ds(rows - 1, freqs, stride=rows)
            moved[j, low_at, :] = moved[j, low_at, :] + low_flux
            moved[j, high_at, :] = moved[j, high_at, :] - high_flux
            fixed = []
            for i in range(3):
                low_sum = jnp.sum(weights[i] * low_flux, axis=0, keepdims=True)
                high_sum = jnp.sum(weights[i] * high_flux, axis=0, keepdims=True)
                fixed.append(
                    sums[j, i]
                    + jnp.where(row_id == 0, low_sum, 0.0)
                    - jnp.where(row_id == rows - 1, high_sum, 0.0)
                )
            two, three, four = fixed
            gain = growth * jnp.maximum(wind_x * cosine + wind_y * sine, 0.0)
            gain_ref[j] = gain
            moment = moment + two
            stress = gain * two
            stress_x = stress_x + cosine * stress
            stress_y = stress_y + sine * stress
            base = three + gain * four
            base_x = base_x + cosine * base
            base_y = base_y + sine * base
            damp_x = damp_x + cosine * four
            damp_y = damp_y + sine * four

    pairs = (
        (STRESS_SCALE * stress_x, zero),
        (STRESS_SCALE * stress_y, zero),
        (STOKES_SCALE * base_x, STOKES_SCALE * damp_x),
        (STOKES_SCALE * base_y, STOKES_SCALE * damp_y),
    )
    for comp in range(4):
        part[comp, 0] = moment
        part[comp, 1] = pairs[comp][0]
        part[comp, 2] = pairs[comp][1]

    def part_copy(to, src, slot):
        return pltpu.make_async_remote_copy(
            src_ref=part.at[to], dst_ref=part_in.at[src], send_sem=part_send.at[slot],
            recv_sem=part_recv.at[src], device_id=(b, to), device_id_type=MESH,
        )

    for o in range(1, bands):
        part_copy(lax.rem(d + o, bands), d, o).start()
    part_in[d] = part[d]
    for o in range(1, bands):
        src = lax.rem(d + o, bands)
        part_copy(src, src, o).wait_recv()
    summed = part_in[0]
    for i in range(1, bands):
        summed = summed + part_in[i]
    steepness = STEEP_COEF * summed[0]
    damping = DAMP_RATE * steepness / (1.0 + steepness)
    for j in range(dirs):
        gain_ref[j] = gain_ref[j] - damping
    force = summed[1] - damping * summed[2]

    square_tile = jnp.concatenate([force, jnp.zeros((LANES - rows, LANES), jnp.float32)], axis=0)
    per_tile = LANES // rows
    stage[...] = jnp.transpose(
        pltpu.roll(square_tile, lax.rem(b, per_tile) * rows, 0)
    )
    if yrows % 8 == 0:
        def force_src(i):
            return stage.at[pl.ds(pl.multiple_of(i * yrows, 8), yrows)]
    else:
        def force_src(i):
            return force_in.at[blocks + i]

        def lay_force(i, carry):
            force_in[blocks + i] = stage[pl.ds(i * yrows, yrows), :]
            return carry

        lax.fori_loop(0, blocks, lay_force, 0)

    def force_copy(to, src, slot):
        return pltpu.make_async_remote_copy(
            src_ref=force_src(to), dst_ref=force_in.at[src], send_sem=force_send.at[slot],
            recv_sem=force_recv.at[src], device_id=(to, d), device_id_type=MESH,
        )

    def send_force(o, carry):
        force_copy(lax.rem(b + o, blocks), b, o).start()
        return carry

    def wait_force(o, carry):
        src = lax.rem(b + o, blocks)
        force_copy(src, src, o).wait_recv()
        return carry

    lax.fori_loop(1, blocks, send_force, 0)
    force_in[b] = stage[pl.ds(b * yrows if yrows % 8 else pl.multiple_of(b * yrows, 8), yrows), :]

    def drain(o, carry):
        to = lax.rem(b + o, blocks)
        ocean_copy(to, b, o).wait_send()
        wind_copy(to, b, o).wait_send()
        ice_copy(to, b, o).wait_send()
        return carry

    lax.fori_loop(1, blocks, drain, 0)
    for side, has in sends:
        @pl.when(has)
        def _(side=side):
            side_copy(side).wait_send()
            for c in range(chunks):
                edge_copy(side, c).wait_send()
    for o in range(1, bands):
        part_copy(lax.rem(d + o, bands), d, o).wait_send()

    lax.fori_loop(1, blocks, wait_force, 0)
    for t in range(blocks // per_tile):
        tile = force_in[t * per_tile]
        for i in range(1, per_tile):
            tile = tile + force_in[t * per_tile + i]
        force_ref[0, :, t * LANES : (t + 1) * LANES] = tile

    def drain_force(o, carry):
        force_copy(lax.rem(b + o, blocks), b, o).wait_send()
        return carry

    lax.fori_loop(1, blocks, drain_force, 0)


def on_device(spectrum, group_speed, ocean_current, route_slot, wind_vector, ice_cover):
    blocks = lax.axis_size("blk")
    bands = lax.axis_size("dir")
    dirs, freqs, rows, width = spectrum.shape
    yrows = ocean_current.shape[1]
    capacity = rows * width // blocks
    wide = max(capacity, LANES)
    chunk = 3 if dirs % 3 == 0 else 1
    chunks = dirs // chunk
    high = blocks * (wide // LANES)
    total = blocks * rows
    padded = (freqs // 8 + 1) * 8
    f32 = jnp.float32
    ratios = RATIO_STEP ** (np.arange(freqs) - (freqs - 1.0))
    shape = (blocks, bands, dirs, freqs, rows, yrows, chunk)
    vmem = pl.BlockSpec(memory_space=pltpu.VMEM)
    hbm = pl.BlockSpec(memory_space=pltpu.HBM)
    dma = pltpu.SemaphoreType.DMA
    force_slots = blocks if yrows % 8 == 0 else 2 * blocks
    moved, net, forcing = pl.pallas_call(
        functools.partial(moved_and_sums, shape),
        out_shape=(
            pltpu.VMEM((dirs, freqs * rows, width), f32),
            pltpu.VMEM((dirs, rows, width), f32),
            pltpu.VMEM((1, yrows, total), f32),
        ),
        in_specs=[hbm] * 6,
        out_specs=(vmem, vmem, vmem),
        scratch_shapes=[
            pltpu.SMEM((2, dirs), f32),
            pltpu.SMEM((3, freqs), f32),
            pltpu.VMEM((freqs * rows, width), f32),
            pltpu.VMEM((2, yrows, total), f32),
            pltpu.VMEM((rows, width), jnp.int32),
            pltpu.VMEM((dirs, freqs * rows, width), f32),
            pltpu.VMEM((freqs * rows, width), f32),
            pltpu.VMEM((freqs * rows, width), f32),
            pltpu.VMEM((2, dirs, freqs, width), f32),
            pltpu.VMEM((2, dirs, freqs, width), f32),
            pltpu.VMEM((2, padded, width), f32),
            pltpu.VMEM((2, padded, width), f32),
            pltpu.VMEM((blocks, 2, yrows, total), f32),
            pltpu.VMEM((2, blocks * yrows, total), f32),
            pltpu.VMEM((2, total + 16, width), f32),
            pltpu.VMEM((blocks, 2, wide), f32),
            pltpu.VMEM((blocks, 1, wide), f32),
            pltpu.VMEM((3 * high, LANES), f32),
            pltpu.VMEM((dirs, 3, rows, width), f32),
            pltpu.VMEM((4, 3, rows, width), f32),
            pltpu.VMEM((bands, 3, rows, width), f32),
            pltpu.VMEM((width, LANES), f32),
            pltpu.VMEM((force_slots, yrows, LANES), f32),
            dma((dirs,)), dma((5,)),
            dma((2, chunks)), dma((2, chunks)), dma((2,)), dma((2,)),
            dma((blocks,)), dma((blocks,)), dma((blocks,)), dma((blocks,)),
            dma((blocks,)), dma((blocks,)),
            dma((bands,)), dma((bands,)), dma((blocks,)), dma((blocks,)),
        ],
        compiler_params=pltpu.CompilerParams(
            collective_id=0, has_side_effects=True, vmem_limit_bytes=60 * 1024 * 1024
        ),
        cost_estimate=pl.CostEstimate(
            flops=30 * spectrum.size, bytes_accessed=8 * spectrum.size, transcendentals=0
        ),
    )(
        spectrum.reshape(dirs, freqs * rows, width),
        group_speed.reshape(freqs * rows, width), ocean_current, route_slot, wind_vector, ice_cover,
    )
    growth = jnp.asarray(ratios, f32)[None, :, None, None] * net[:, None]
    result = moved.reshape(dirs, freqs, rows, width) * (1.0 + growth)
    return result, forcing


def solution(mesh):
    return jax.shard_map(
        on_device,
        mesh=mesh,
        in_specs=(
            P("dir", None, "blk", None),
            P(None, "blk", None),
            P(None, "blk", None),
            P("blk", None),
            P("blk", None, None),
            P("blk", None),
        ),
        out_specs=(P("dir", None, "blk", None), P("dir", "blk", None)),
        check_vma=False,
    )
```

```python
import functools
import math

import jax
import jax.numpy as jnp
import numpy as np
from jax import lax
from jax.experimental import pallas as pl
from jax.experimental.pallas import tpu as pltpu
from jax.sharding import PartitionSpec as P

COURANT = 0.15
WIND_GROWTH = 0.15
DAMP_RATE = 0.5
STEEP_COEF = 0.01
STRESS_SCALE = 1.0
STOKES_SCALE = 0.15
RATIO_STEP = 1.1
LANES = 128
MESH = pl.DeviceIdType.MESH


def moved_and_sums(
    shape,
    spec_hbm, speed_hbm, ocean_hbm, route_hbm, wind_ref, ice_ref,
    moved, gain_ref, force_ref,
    trig_ref, ratio_ref, speed_ref, ocean_ref, route_ref,
    spec, face_x, face_y, edge_out, edge_in, side_out, side_in,
    ocean_in, ocean_yx, ocean_xy, wind_in, ice_in, table, sums, part, part_in, stage, force_in,
    load_sem, small_sem, edge_send, edge_recv, side_send, side_recv,
    ocean_send, ocean_recv, wind_send, wind_recv, ice_send, ice_recv,
    part_send, part_recv, force_send, force_recv,
):
    blocks, bands, dirs, freqs, rows, yrows, chunk = shape
    width = rows * freqs
    b = lax.axis_index("blk")
    d = lax.axis_index("dir")
    capacity = rows * LANES // blocks
    wide = max(capacity, LANES)
    tiles = wide // LANES
    chunks = dirs // chunk

    def load(j):
        return pltpu.make_async_copy(spec_hbm.at[j], spec.at[j], load_sem.at[j])

    small = [
        pltpu.make_async_copy(speed_hbm, speed_ref, small_sem.at[0]),
        pltpu.make_async_copy(route_hbm, route_ref, small_sem.at[1]),
        pltpu.make_async_copy(ocean_hbm, ocean_ref, small_sem.at[2]),
    ]
    for copy in small:
        copy.start()
    for j in range(dirs):
        load(j).start()
    own_lane = pl.multiple_of(((b * capacity) // LANES) * LANES, LANES)
    own_wind = pltpu.make_async_copy(
        wind_ref.at[0, :, pl.ds(own_lane, wide)], wind_in.at[b], small_sem.at[3]
    )
    own_ice = pltpu.make_async_copy(
        ice_ref.at[:, pl.ds(own_lane, wide)], ice_in.at[b], small_sem.at[4]
    )
    own_wind.start()
    own_ice.start()

    barrier = pltpu.get_barrier_semaphore()

    def greet_blk(o, carry):
        pl.semaphore_signal(
            barrier, inc=1, device_id=(lax.rem(b + o, blocks), d), device_id_type=MESH
        )
        return carry

    lax.fori_loop(1, blocks, greet_blk, 0, unroll=blocks <= 16)
    for o in range(1, bands):
        pl.semaphore_signal(
            barrier, inc=1, device_id=(b, lax.rem(d + o, bands)), device_id_type=MESH
        )

    count = dirs * bands
    for j in range(dirs):
        for i, wave in enumerate((math.cos, math.sin)):
            value = jnp.float32(wave(2.0 * math.pi * j / count))
            for band in range(1, bands):
                angle = 2.0 * math.pi * (band * dirs + j) / count
                value = jnp.where(d == band, jnp.float32(wave(angle)), value)
            trig_ref[i, j] = value
    for k in range(freqs):
        for i in range(3):
            ratio_ref[i, k] = jnp.float32(RATIO_STEP ** ((k - freqs + 1.0) * (i + 2)))

    for copy in small:
        copy.wait()
    sea = jnp.where(route_ref[...] >= 0, 1.0, 0.0).astype(jnp.float32)
    for side, row in ((0, rows - 1), (1, 0)):
        side_out[side, :freqs, :] = speed_ref[pl.ds(row, freqs, stride=rows), :]
        side_out[side, freqs : freqs + 1, :] = sea[row : row + 1, :]

    @pl.when(b == 0)
    def _():
        side_in[0] = jnp.zeros_like(side_in[0])
        edge_in[0] = jnp.zeros_like(edge_in[0])

    @pl.when(b == blocks - 1)
    def _():
        side_in[1] = jnp.zeros_like(side_in[1])
        edge_in[1] = jnp.zeros_like(edge_in[1])

    pl.semaphore_wait(barrier, blocks - 1 + bands - 1)

    def ocean_copy(to, src, slot):
        return pltpu.make_async_remote_copy(
            src_ref=ocean_hbm, dst_ref=ocean_in.at[src], send_sem=ocean_send.at[slot],
            recv_sem=ocean_recv.at[src], device_id=(to, d), device_id_type=MESH,
        )

    def wind_copy(to, src, slot):
        start = pl.multiple_of(((to * capacity) // LANES) * LANES, LANES)
        return pltpu.make_async_remote_copy(
            src_ref=wind_ref.at[0, :, pl.ds(start, wide)], dst_ref=wind_in.at[src],
            send_sem=wind_send.at[slot], recv_sem=wind_recv.at[src],
            device_id=(to, d), device_id_type=MESH,
        )

    def ice_copy(to, src, slot):
        start = pl.multiple_of(((to * capacity) // LANES) * LANES, LANES)
        return pltpu.make_async_remote_copy(
            src_ref=ice_ref.at[:, pl.ds(start, wide)], dst_ref=ice_in.at[src],
            send_sem=ice_send.at[slot], recv_sem=ice_recv.at[src],
            device_id=(to, d), device_id_type=MESH,
        )

    def send_ocean(o, carry):
        ocean_copy(lax.rem(b + o, blocks), b, o).start()
        return carry

    def send_winds(o, carry):
        to = lax.rem(b + o, blocks)
        wind_copy(to, b, o).start()
        ice_copy(to, b, o).start()
        return carry

    lax.fori_loop(1, blocks, send_ocean, 0, unroll=blocks <= 16)

    def side_copy(side):
        return pltpu.make_async_remote_copy(
            src_ref=side_out.at[side], dst_ref=side_in.at[side], send_sem=side_send.at[side],
            recv_sem=side_recv.at[side], device_id=(b + 1 - 2 * side, d), device_id_type=MESH,
        )

    def edge_copy(side, c):
        part_of = pl.ds(c * chunk, chunk)
        return pltpu.make_async_remote_copy(
            src_ref=edge_out.at[side, part_of], dst_ref=edge_in.at[side, part_of],
            send_sem=edge_send.at[side, c], recv_sem=edge_recv.at[side, c],
            device_id=(b + 1 - 2 * side, d), device_id_type=MESH,
        )

    sends = ((0, b < blocks - 1), (1, b > 0))
    receives = ((0, b > 0), (1, b < blocks - 1))
    for side, has in sends:
        @pl.when(has)
        def _(side=side):
            side_copy(side).start()

    for c in range(chunks):
        for j in range(c * chunk, (c + 1) * chunk):
            load(j).wait()
            for side, row in ((0, rows - 1), (1, 0)):
                edge_out[side, j] = spec[j, pl.ds(row, freqs, stride=rows), :]
        for side, has in sends:
            @pl.when(has)
            def _(side=side, c=c):
                edge_copy(side, c).start()

    lax.fori_loop(1, blocks, send_winds, 0, unroll=blocks <= 16)

    row_id = lax.broadcasted_iota(jnp.int32, (rows, LANES), 0)
    lane_id = lax.broadcasted_iota(jnp.int32, (rows, LANES), 1)

    def next_row(value):
        return pltpu.roll(value, rows - 1, 0)

    def next_lane(value):
        return pltpu.roll(value, LANES - 1, 1)

    half = 0.5 * COURANT
    open_x = jnp.where(row_id < rows - 1, half * sea * next_row(sea), 0.0)
    open_y = jnp.where(lane_id < LANES - 1, half * sea * next_lane(sea), 0.0)

    def faces(k, carry):
        at = pl.ds(pl.multiple_of(k * rows, rows), rows)
        speed = speed_ref[at, :]
        face_x[at, :] = open_x * (speed + next_row(speed))
        face_y[at, :] = open_y * (speed + next_lane(speed))
        return carry

    lax.fori_loop(0, freqs, faces, 0, unroll=4)

    ocean_in[b] = ocean_ref[...]

    def wait_ocean(o, carry):
        ocean_copy(lax.rem(b + o, blocks), lax.rem(b + o, blocks), o).wait_recv()
        return carry

    lax.fori_loop(1, blocks, wait_ocean, 0, unroll=blocks <= 16)

    def lay_ocean(i, carry):
        at = i * yrows
        if yrows % 8 == 0:
            at = pl.multiple_of(at, 8)
        for comp in range(2):
            ocean_yx[comp, pl.ds(at, yrows), :] = ocean_in[i, comp]
        return carry

    lax.fori_loop(0, blocks, lay_ocean, 0, unroll=blocks <= 16)
    ocean_xy[:, 0:8, :] = jnp.zeros((2, 8, LANES), jnp.float32)
    total = blocks * rows
    ocean_xy[:, total + 8 : total + 16, :] = jnp.zeros((2, 8, LANES), jnp.float32)
    for comp in range(2):
        for t in range(total // LANES):
            ocean_xy[comp, 8 + t * LANES : 8 + (t + 1) * LANES, :] = jnp.transpose(
                ocean_yx[comp, :, t * LANES : (t + 1) * LANES]
            )
    own = pl.ds(pl.multiple_of(b * rows + 8, 8), rows)
    flow_x = ocean_xy[0, own, :]
    flow_y = ocean_xy[1, own, :]
    flow_low = ocean_xy[0, pl.ds(b * rows + 7, 1), :]
    flow_high = ocean_xy[0, pl.ds(b * rows + 8 + rows, 1), :]
    cur_x = open_x * (flow_x + next_row(flow_x))
    cur_y = open_y * (flow_y + next_lane(flow_y))

    group = 1
    for size in (18, 12, 9, 6, 4, 3, 2):
        if freqs % size == 0:
            group = size
            break

    def one_dir(j, carry):
        cosine = trig_ref[0, j]
        sine = trig_ref[1, j]

        def some_freqs(g, acc):
            two, three, four = acc
            for i in range(group):
                k = g * group + i
                at = pl.ds(pl.multiple_of(k * rows, rows), rows)
                energy = spec[j, at, :]
                speed_x = face_x[at, :] * cosine + cur_x
                flux_x = speed_x * jnp.where(speed_x > 0.0, energy, next_row(energy))
                speed_y = face_y[at, :] * sine + cur_y
                flux_y = speed_y * jnp.where(speed_y > 0.0, energy, next_lane(energy))
                value = (
                    sea * energy - (flux_x - pltpu.roll(flux_x, 1, 0))
                ) - (flux_y - pltpu.roll(flux_y, 1, 1))
                moved[j, at, :] = value
                two = two + ratio_ref[0, k] * value
                three = three + ratio_ref[1, k] * value
                four = four + ratio_ref[2, k] * value
            return two, three, four

        zero = jnp.zeros((rows, LANES), jnp.float32)
        acc = lax.fori_loop(0, freqs // group, some_freqs, (zero, zero, zero))
        for i in range(3):
            sums[j, i] = acc[i]
        return carry

    lax.fori_loop(0, dirs, one_dir, 0)

    high = blocks * tiles
    own_wind.wait()
    own_ice.wait()

    def wait_winds(o, carry):
        src = lax.rem(b + o, blocks)
        wind_copy(src, src, o).wait_recv()
        ice_copy(src, src, o).wait_recv()
        return carry

    lax.fori_loop(1, blocks, wait_winds, 0, unroll=blocks <= 16)

    def lay_table(i, carry):
        for t in range(tiles):
            lanes = slice(t * LANES, (t + 1) * LANES)
            for comp in range(2):
                table[pl.ds(comp * high + i * tiles + t, 1), :] = wind_in[i, comp : comp + 1, lanes]
            table[pl.ds(2 * high + i * tiles + t, 1), :] = ice_in[i, :, lanes]
        return carry

    lax.fori_loop(0, blocks, lay_table, 0, unroll=blocks <= 16)
    whole = table[...]
    first = whole.astype(jnp.bfloat16)
    rest = whole - first.astype(jnp.float32)
    second = rest.astype(jnp.bfloat16)
    third = (rest - second.astype(jnp.float32)).astype(jnp.bfloat16)
    entry_id = lax.broadcasted_iota(jnp.int32, (LANES, LANES), 0)
    high_id = lax.broadcasted_iota(jnp.int32, (high, LANES), 0)
    per_row = int(math.log2(min(capacity, LANES)))
    offset = lax.rem(b * capacity, LANES) if capacity < LANES else 0
    found = [[], [], []]
    for row in range(rows):
        slot = route_ref[row : row + 1, :]
        upper = lax.shift_right_arithmetic(slot, per_row)
        lower = jnp.bitwise_and(slot, (1 << per_row) - 1) + offset
        hot = jnp.where(entry_id == lower, 1.0, 0.0).astype(jnp.bfloat16)
        values = sum(
            jnp.dot(piece, hot, preferred_element_type=jnp.float32)
            for piece in (third, second, first)
        )
        here = high_id == upper
        for i in range(3):
            found[i].append(
                jnp.sum(
                    jnp.where(here, values[i * high : (i + 1) * high], 0.0), axis=0, keepdims=True
                )
            )
    wind_x, wind_y, ice = (jnp.concatenate(value, axis=0) for value in found)
    growth = WIND_GROWTH * (1.0 - ice)

    for side, has in receives:
        @pl.when(has)
        def _(side=side):
            side_copy(side).wait_recv()
    low_open = half * side_in[0, freqs : freqs + 1, :] * sea[0:1]
    high_open = half * side_in[1, freqs : freqs + 1, :] * sea[rows - 1 : rows]
    low_face = low_open * (side_in[0, :freqs, :] + side_out[1, :freqs, :])
    high_face = high_open * (side_in[1, :freqs, :] + side_out[0, :freqs, :])
    low_cur = low_open * (flow_low + flow_x[0:1])
    high_cur = high_open * (flow_high + flow_x[rows - 1 : rows])
    power = lax.broadcasted_iota(jnp.int32, (freqs, LANES), 0).astype(jnp.float32) - (freqs - 1)
    ratio = jnp.exp(power * math.log(RATIO_STEP))
    square = ratio * ratio
    weights = (square, square * ratio, square * square)

    zero = jnp.zeros((rows, LANES), jnp.float32)
    moment, stress_x, stress_y, base_x, base_y, damp_x, damp_y = [zero] * 7
    for c in range(chunks):
        for side, has in receives:
            @pl.when(has)
            def _(side=side, c=c):
                edge_copy(side, c).wait_recv()
        for j in range(c * chunk, (c + 1) * chunk):
            cosine = trig_ref[0, j]
            sine = trig_ref[1, j]
            low_speed = low_face * cosine + low_cur
            high_speed = high_face * cosine + high_cur
            low_flux = low_speed * jnp.where(low_speed > 0.0, edge_in[0, j], edge_out[1, j])
            high_flux = high_speed * jnp.where(high_speed > 0.0, edge_out[0, j], edge_in[1, j])
            low_at = pl.ds(0, freqs, stride=rows)
            high_at = pl.ds(rows - 1, freqs, stride=rows)
            moved[j, low_at, :] = moved[j, low_at, :] + low_flux
            moved[j, high_at, :] = moved[j, high_at, :] - high_flux
            fixed = []
            for i in range(3):
                low_sum = jnp.sum(weights[i] * low_flux, axis=0, keepdims=True)
                high_sum = jnp.sum(weights[i] * high_flux, axis=0, keepdims=True)
                fixed.append(
                    sums[j, i]
                    + jnp.where(row_id == 0, low_sum, 0.0)
                    - jnp.where(row_id == rows - 1, high_sum, 0.0)
                )
            two, three, four = fixed
            gain = growth * jnp.maximum(wind_x * cosine + wind_y * sine, 0.0)
            gain_ref[j] = gain
            moment = moment + two
            stress = gain * two
            stress_x = stress_x + cosine * stress
            stress_y = stress_y + sine * stress
            base = three + gain * four
            base_x = base_x + cosine * base
            base_y = base_y + sine * base
            damp_x = damp_x + cosine * four
            damp_y = damp_y + sine * four

    pairs = (
        (STRESS_SCALE * stress_x, zero),
        (STRESS_SCALE * stress_y, zero),
        (STOKES_SCALE * base_x, STOKES_SCALE * damp_x),
        (STOKES_SCALE * base_y, STOKES_SCALE * damp_y),
    )
    for comp in range(4):
        part[comp, 0] = moment
        part[comp, 1] = pairs[comp][0]
        part[comp, 2] = pairs[comp][1]

    def part_copy(to, src, slot):
        return pltpu.make_async_remote_copy(
            src_ref=part.at[to], dst_ref=part_in.at[src], send_sem=part_send.at[slot],
            recv_sem=part_recv.at[src], device_id=(b, to), device_id_type=MESH,
        )

    for o in range(1, bands):
        part_copy(lax.rem(d + o, bands), d, o).start()
    part_in[d] = part[d]
    for o in range(1, bands):
        src = lax.rem(d + o, bands)
        part_copy(src, src, o).wait_recv()
    summed = part_in[0]
    for i in range(1, bands):
        summed = summed + part_in[i]
    steepness = STEEP_COEF * summed[0]
    damping = DAMP_RATE * steepness / (1.0 + steepness)
    for j in range(dirs):
        gain_ref[j] = gain_ref[j] - damping
    force = summed[1] - damping * summed[2]

    square_tile = jnp.concatenate([force, jnp.zeros((LANES - rows, LANES), jnp.float32)], axis=0)
    per_tile = LANES // rows
    stage[...] = jnp.transpose(
        pltpu.roll(square_tile, lax.rem(b, per_tile) * rows, 0)
    )
    if yrows % 8 == 0:
        def force_src(i):
            return stage.at[pl.ds(pl.multiple_of(i * yrows, 8), yrows)]
    else:
        def force_src(i):
            return force_in.at[blocks + i]

        def lay_force(i, carry):
            force_in[blocks + i] = stage[pl.ds(i * yrows, yrows), :]
            return carry

        lax.fori_loop(0, blocks, lay_force, 0)

    def force_copy(to, src, slot):
        return pltpu.make_async_remote_copy(
            src_ref=force_src(to), dst_ref=force_in.at[src], send_sem=force_send.at[slot],
            recv_sem=force_recv.at[src], device_id=(to, d), device_id_type=MESH,
        )

    def send_force(o, carry):
        force_copy(lax.rem(b + o, blocks), b, o).start()
        return carry

    def wait_force(o, carry):
        src = lax.rem(b + o, blocks)
        force_copy(src, src, o).wait_recv()
        return carry

    lax.fori_loop(1, blocks, send_force, 0, unroll=blocks <= 16)
    force_in[b] = stage[pl.ds(b * yrows if yrows % 8 else pl.multiple_of(b * yrows, 8), yrows), :]

    def drain(o, carry):
        to = lax.rem(b + o, blocks)
        ocean_copy(to, b, o).wait_send()
        wind_copy(to, b, o).wait_send()
        ice_copy(to, b, o).wait_send()
        return carry

    lax.fori_loop(1, blocks, drain, 0, unroll=blocks <= 16)
    for side, has in sends:
        @pl.when(has)
        def _(side=side):
            side_copy(side).wait_send()
            for c in range(chunks):
                edge_copy(side, c).wait_send()
    for o in range(1, bands):
        part_copy(lax.rem(d + o, bands), d, o).wait_send()

    lax.fori_loop(1, blocks, wait_force, 0, unroll=blocks <= 16)
    for t in range(blocks // per_tile):
        tile = force_in[t * per_tile]
        for i in range(1, per_tile):
            tile = tile + force_in[t * per_tile + i]
        force_ref[0, :, t * LANES : (t + 1) * LANES] = tile

    def drain_force(o, carry):
        force_copy(lax.rem(b + o, blocks), b, o).wait_send()
        return carry

    lax.fori_loop(1, blocks, drain_force, 0, unroll=blocks <= 16)


def finish(ratios, moved, net, force, result_hbm, force_out, buffer, done):
    dirs, freqs, rows = moved.shape[0], len(ratios), net.shape[1]

    def store(j, slot):
        return pltpu.make_async_copy(buffer.at[slot], result_hbm.at[j], done.at[slot])

    force_out[...] = force[...]
    for j in range(dirs):
        gain = net[j]
        for k in range(freqs):
            at = slice(k * rows, (k + 1) * rows)
            buffer[j, at, :] = moved[j, at, :] * (1.0 + ratios[k] * gain)
        store(j, j).start()
    for j in range(dirs):
        store(j, j).wait()


def on_device(spectrum, group_speed, ocean_current, route_slot, wind_vector, ice_cover):
    blocks = lax.axis_size("blk")
    bands = lax.axis_size("dir")
    dirs, freqs, rows, width = spectrum.shape
    yrows = ocean_current.shape[1]
    capacity = rows * width // blocks
    wide = max(capacity, LANES)
    chunk = 3 if dirs % 3 == 0 else 1
    chunks = dirs // chunk
    high = blocks * (wide // LANES)
    total = blocks * rows
    padded = (freqs // 8 + 1) * 8
    f32 = jnp.float32
    ratios = RATIO_STEP ** (np.arange(freqs) - (freqs - 1.0))
    shape = (blocks, bands, dirs, freqs, rows, yrows, chunk)
    vmem = pl.BlockSpec(memory_space=pltpu.VMEM)
    hbm = pl.BlockSpec(memory_space=pltpu.HBM)
    dma = pltpu.SemaphoreType.DMA
    force_slots = blocks if yrows % 8 == 0 else 2 * blocks
    moved, net, forcing = pl.pallas_call(
        functools.partial(moved_and_sums, shape),
        out_shape=(
            pltpu.VMEM((dirs, freqs * rows, width), f32),
            pltpu.VMEM((dirs, rows, width), f32),
            pltpu.VMEM((1, yrows, total), f32),
        ),
        in_specs=[hbm] * 6,
        out_specs=(vmem, vmem, vmem),
        scratch_shapes=[
            pltpu.SMEM((2, dirs), f32),
            pltpu.SMEM((3, freqs), f32),
            pltpu.VMEM((freqs * rows, width), f32),
            pltpu.VMEM((2, yrows, total), f32),
            pltpu.VMEM((rows, width), jnp.int32),
            pltpu.VMEM((dirs, freqs * rows, width), f32),
            pltpu.VMEM((freqs * rows, width), f32),
            pltpu.VMEM((freqs * rows, width), f32),
            pltpu.VMEM((2, dirs, freqs, width), f32),
            pltpu.VMEM((2, dirs, freqs, width), f32),
            pltpu.VMEM((2, padded, width), f32),
            pltpu.VMEM((2, padded, width), f32),
            pltpu.VMEM((blocks, 2, yrows, total), f32),
            pltpu.VMEM((2, blocks * yrows, total), f32),
            pltpu.VMEM((2, total + 16, width), f32),
            pltpu.VMEM((blocks, 2, wide), f32),
            pltpu.VMEM((blocks, 1, wide), f32),
            pltpu.VMEM((3 * high, LANES), f32),
            pltpu.VMEM((dirs, 3, rows, width), f32),
            pltpu.VMEM((4, 3, rows, width), f32),
            pltpu.VMEM((bands, 3, rows, width), f32),
            pltpu.VMEM((width, LANES), f32),
            pltpu.VMEM((force_slots, yrows, LANES), f32),
            dma((dirs,)), dma((5,)),
            dma((2, chunks)), dma((2, chunks)), dma((2,)), dma((2,)),
            dma((blocks,)), dma((blocks,)), dma((blocks,)), dma((blocks,)),
            dma((blocks,)), dma((blocks,)),
            dma((bands,)), dma((bands,)), dma((blocks,)), dma((blocks,)),
        ],
        compiler_params=pltpu.CompilerParams(
            collective_id=0, has_side_effects=True, vmem_limit_bytes=60 * 1024 * 1024
        ),
        cost_estimate=pl.CostEstimate(
            flops=30 * spectrum.size, bytes_accessed=8 * spectrum.size, transcendentals=0
        ),
    )(
        spectrum.reshape(dirs, freqs * rows, width),
        group_speed.reshape(freqs * rows, width), ocean_current, route_slot, wind_vector, ice_cover,
    )
    result, forcing = pl.pallas_call(
        functools.partial(finish, [float(ratio) for ratio in ratios]),
        out_shape=(
            jax.ShapeDtypeStruct((dirs, freqs * rows, width), f32),
            jax.ShapeDtypeStruct((1, yrows, total), f32),
        ),
        in_specs=[vmem, vmem, vmem],
        out_specs=(hbm, vmem),
        scratch_shapes=[pltpu.VMEM((dirs, freqs * rows, width), f32), dma((dirs,))],
        compiler_params=pltpu.CompilerParams(vmem_limit_bytes=16 * 1024 * 1024),
    )(moved, net, forcing)
    return result.reshape(dirs, freqs, rows, width), forcing


def solution(mesh):
    return jax.shard_map(
        on_device,
        mesh=mesh,
        in_specs=(
            P("dir", None, "blk", None),
            P(None, "blk", None),
            P(None, "blk", None),
            P("blk", None),
            P("blk", None, None),
            P("blk", None),
        ),
        out_specs=(P("dir", None, "blk", None), P("dir", "blk", None)),
        check_vma=False,
    )
```
